512 devices in a mesh: ex: 8 (over z_lo, x), blk: 64 (over z_hi, y, core).
Axes of the slice: x: 4, y: 8, z: 8 (z_hi: 4, z_lo: 2; z = z_hi * 2 + z_lo), core: 2. Of those that a mesh axis runs over, the one named last changes fastest.
Arguments:
- activations: bfloat16 [1024, 28672], P('blk', 'ex'), may hold values from -6 to 6
- out_grads: bfloat16 [1024, 8192], P('ex', 'blk'), may hold values from -0.5 to 0.5
- basis_in: bfloat16 [28672, 28672], P('ex', 'blk'), may hold values from -0.03125 to 0.03125
- basis_out: bfloat16 [8192, 4096], P('blk', 'ex'), may hold values from -0.0625 to 0.0625
- example_ids: int32 [1024], replicated, may hold values from 0 to 8, as said below
Outputs:
- correction: float32 [4096, 28672], P('ex', 'blk')
The draws below stay inside these ranges and needn't reach their ends.
Inputs may be any that keep to these rules, and one draw needn't show every extreme that they name: `example_ids`: example ids never fall along the tokens; every example 0 to 7 holds 1 to 192 tokens, and some example exactly 192; the id 8 marks padding tokens after the last example.
All inputs are finite; a program needn't handle non-finite values.
Results may differ from the reference program's by a relative error of at most 0.0029.
Values may be sent and summed in bfloat16 or wider, within the bound.
A program may use at most 64 MiB of HBM per device.

```python
import jax
import jax.numpy as jnp
from jax import lax

F = 28672
OUT = 8192
OUTW = 4096
EXAMPLES = 8
TOKENS = 1024
MOST = 192


def draw_example_ids(key, part):
    key_place = jax.random.fold_in(key, 11)
    key_lengths = jax.random.fold_in(key, 23)
    others = EXAMPLES - 1
    remain = TOKENS - MOST
    most_other = remain // others
    least_other = max(1, most_other // 2)
    other_lengths = jax.random.randint(key_lengths, (others,), least_other, most_other + 1).astype(jnp.int32)
    chosen = jax.random.randint(key_place, (), 0, EXAMPLES).astype(jnp.int32)
    position = jnp.arange(EXAMPLES, dtype=jnp.int32)
    before = other_lengths[jnp.clip(position, 0, others - 1)]
    after = other_lengths[jnp.clip(position - 1, 0, others - 1)]
    lengths = jnp.where(position < chosen, before, jnp.where(position == chosen, MOST, after)).astype(jnp.int32)
    ends = jnp.cumsum(lengths).astype(jnp.int32)
    tokens_at = jnp.arange(TOKENS, dtype=jnp.int32)
    return jnp.sum((ends[None, :] <= tokens_at[:, None]).astype(jnp.int32), axis=1).astype(jnp.int32)


def block_levels(stream_key, shape, cuts, smallest, largest):
    def one(axis_at, shards_of):
        steps = jax.random.uniform(jax.random.fold_in(jax.random.fold_in(stream_key, 6), axis_at), (shards_of,), jnp.float32, smallest / len(cuts), largest / len(cuts))
        return jnp.repeat(jnp.exp(steps), shape[axis_at] // shards_of).reshape((-1,) + (1,) * (len(shape) - axis_at - 1))

    factor_of = one(*cuts[0])
    for cut in cuts[1:]:
        factor_of = factor_of * one(*cut)
    return factor_of


def centred(rng, dims, width, most, pieces=(), kind=jnp.bfloat16):
    array = jax.random.normal(rng, dims, jnp.float32) * width
    if len(pieces) > 0:
        array = block_levels(rng, dims, pieces, -0.22, 0.18) * array
    return jnp.clip(array, min=-most, max=most).astype(kind)


def setup_inputs(seed: int = 0) -> dict:
    keys = jax.random.split(jax.random.key(seed), 6)
    activations = centred(keys[0], (TOKENS, F), 1.0, 6.0, ((0, 64), (1, 8)))
    out_grads = centred(keys[1], (TOKENS, OUT), 0.0625, 0.5, ((0, 8), (1, 64)))
    basis_in = centred(keys[2], (F, F), F ** -0.5, 0.03125, ((0, 8), (1, 64)))
    basis_out = centred(keys[3], (OUT, OUTW), OUT ** -0.5, 0.0625, ((0, 64), (1, 8)))
    example_ids = draw_example_ids(jax.random.fold_in(keys[5], 71), 0)
    return {"activations": activations, "out_grads": out_grads, "basis_in": basis_in, "basis_out": basis_out, "example_ids": example_ids}


def reference(activations, out_grads, basis_in, basis_out, example_ids):
    proj_in = jnp.dot(activations, basis_in, preferred_element_type=jnp.float32).astype(jnp.bfloat16)
    proj_out = jnp.dot(out_grads, basis_out, preferred_element_type=jnp.float32).astype(jnp.bfloat16)

    def add_example(example, running):
        offset = jnp.sum((example_ids < example).astype(jnp.int32))
        window_start = jnp.minimum(offset, TOKENS - MOST).astype(jnp.int32)
        window_ids = lax.dynamic_slice_in_dim(example_ids, window_start, MOST, 0)
        chosen = (window_ids == example).astype(proj_out.dtype)
        out_window = lax.dynamic_slice_in_dim(proj_out, window_start, MOST, 0) * chosen[:, None]
        in_window = lax.dynamic_slice_in_dim(proj_in, window_start, MOST, 0)
        example_grad = lax.dot_general(out_window, in_window, (((0,), (0,)), ((), ())), preferred_element_type=jnp.float32)
        return running + example_grad * example_grad

    running = lax.fori_loop(0, EXAMPLES, add_example, jnp.zeros((OUTW, F), jnp.float32))
    return running / EXAMPLES
```

```python
import functools

import jax
import jax.numpy as jnp
from jax import lax
from jax.experimental import pallas as pl
from jax.experimental.pallas import tpu as pltpu
from jax.sharding import Mesh
from jax.sharding import PartitionSpec as P

AXES = ("zl", "x", "zh", "y", "c")
EX = ("zl", "x")
BLK = ("zh", "y", "c")
MESH = pl.DeviceIdType.MESH
MOST = 192
NX, NY, NZ, NE = 4, 8, 4, 8
ROWS = 16
BF = jnp.bfloat16
F32 = jnp.float32

Y_RATE = 46e3
Z_RATE = 23e3
X_RATE = 46e3
D_RATE = 600e3
LAG = 1.6


class Message:
    def __init__(self, link, nbytes, make, whole=None):
        self.link, self.nbytes, self.make, self.whole = link, nbytes, make, whole
        self.copies = None


class Task:
    def __init__(self, needs, sends, run=None, cost=0.05, after=(), rank=0):
        self.needs, self.sends, self.run = needs, sends, run
        self.cost, self.after, self.rank = cost, after, rank


def ordered(tasks, messages):
    rates = {"y+": Y_RATE, "y-": Y_RATE, "z+": Z_RATE, "z-": Z_RATE, "x": X_RATE, "d": D_RATE}
    free = dict.fromkeys(rates, 0.0)
    arrived, done, now, order = {}, {}, 0.0, []
    left = dict(tasks)
    while left:
        best = None
        for name, task in left.items():
            if any(m not in arrived for m in task.needs) or any(t not in done for t in task.after):
                continue
            ready = max([arrived[m] for m in task.needs] + [done[t] for t in task.after] + [0.0])
            key = (max(ready, now), task.rank, ready)
            if best is None or key < best[0]:
                best = (key, name)
        (start, _, _), name = best
        task = left.pop(name)
        now = start + task.cost
        done[name] = now
        for m in task.sends:
            message = messages[m]
            begin = max(now, free[message.link])
            free[message.link] = begin + message.nbytes / rates[message.link]
            arrived[m] = free[message.link] + LAG
        order.append(name)
    return order


def exchange(
    wide1,
    a_ref, g_ref, b_hbm, bo_ref, pi_ref, pall_ref,
    abuf, bbuf, gbuf, bobuf, pp, ring, zown, zbuf, part, mine, rsend, rbuf,
    ssem, rsem, bsem,
):
    zl, x, zh, y, c = (lax.axis_index(n) for n in AXES)
    e = zl * NX + x
    feats = a_ref.shape[1]
    outs = bo_ref.shape[1]
    width = b_hbm.shape[1]
    spans = ((0, wide1), (wide1, feats - wide1))

    def at_y(d):
        return (zl, x, zh, lax.rem(y + d + NY, NY), c)

    def at_z(d):
        return (zl, x, lax.rem(zh + d + NZ, NZ), y, c)

    def at_e(k, other=0):
        ek = lax.rem(e + k, NE)
        return (ek // NX, lax.rem(ek, NX), zh, y, lax.rem(c + other, 2))

    load_b = pltpu.make_async_copy(b_hbm, bbuf, bsem.at[0])
    load_b.start()

    partners = [at_y(1), at_y(-1), at_z(1), at_z(2), at_z(3)]
    partners += [at_e(k, o) for k in range(NE) for o in range(2) if (k, o) != (0, 0)]
    barrier = pltpu.get_barrier_semaphore()
    for device in partners:
        pl.semaphore_signal(barrier, inc=1, device_id=device, device_id_type=MESH)
    pl.semaphore_wait(barrier, len(partners))

    messages, tasks = {}, {}
    counts = [0, 0]

    def message(name, link, nbytes, parts, whole=None):
        arrival = counts[1]
        counts[1] += 1

        def make():
            copies = []
            for src, dst, device in parts():
                copies.append(
                    pltpu.make_async_remote_copy(
                        src_ref=src, dst_ref=dst,
                        send_sem=ssem.at[counts[0]], recv_sem=rsem.at[arrival],
                        device_id=device, device_id_type=MESH,
                    )
                )
                counts[0] += 1
            return copies

        messages[name] = Message(link, nbytes, make, None if whole is None else (whole, arrival))

    def a_slot(color, dy, dz, half=None, own=True):
        at, size = spans[color]
        if half is not None:
            size //= 2
            at += half * size
        cols = pl.ds(at, size)
        if own and (dy, dz) == (0, 0):
            return a_ref.at[:, cols], size
        return abuf.at[dy, 0, dz, :, cols], size

    def a_message(color, dy, dz, axis, sign, half=None):
        sy, sz = ((dy + sign) % NY, dz) if axis == "y" else (dy, (dz + sign) % NZ)
        size = a_slot(color, dy, dz, half)[1]
        device = at_y(sign) if axis == "y" else at_z(sign)
        name = ("a", color, dy, dz, half)
        message(
            name, axis + ("+" if sign > 0 else "-"), ROWS * size * 2,
            lambda: [(a_slot(color, sy, sz, half)[0], a_slot(color, dy, dz, half, False)[0], device)],
        )
        return name

    def along(color, axis, count, fixed):
        steps = {}
        for sign in (1, -1):
            chain = []
            for d in range(1, count // 2 + 1):
                place = (-sign * d) % count
                half = None if d < count // 2 else (0 if sign > 0 else 1)
                dy, dz = (place, fixed) if axis == "y" else (fixed, place)
                chain.append((a_message(color, dy, dz, axis, sign, half), (dy, dz)))
            steps[sign] = chain
        return steps

    first_sends = []
    filled = {(0, 0, 0): [], (1, 0, 0): []}
    starts = {}

    def ring_tasks(color, axis, fixed, from_task, rank):
        steps = along(color, axis, NY if axis == "y" else NZ, fixed)
        for sign in (1, -1):
            chain = steps[sign]
            for (name, place), (following, _) in zip(chain, chain[1:]):
                tasks[("fwd", name)] = Task([name], [following], rank=rank)
            for name, place in chain:
                filled.setdefault((color, *place), []).append(name)
        return [steps[1][0][0], steps[-1][0][0]]

    if True:
        own_sends = []
        own_sends += ring_tasks(0, "z", 0, None, 0)
        for dz in (0, 1, 3, 2):
            sends = ring_tasks(0, "y", dz, None, 1)
            if dz == 0:
                own_sends += sends
            else:
                starts[(0, 0, dz)] = sends
        sends = ring_tasks(1, "y", 0, None, 0)
        own_sends += sends
        for dy in (0, 1, 7, 2, 6, 3, 5, 4):
            sends = ring_tasks(1, "z", dy, None, 1)
            if dy == 0:
                own_sends += sends
            else:
                starts[(1, dy, 0)] = sends
        for place, sends in starts.items():
            tasks[("go", place)] = Task(filled[place], sends, rank=1)

    for dy in range(NY):
        for color in range(2):
            cols = pl.ds(*spans[color])
            piece = lambda slot, dy=dy, cols=cols: abuf.at[dy, slot, :, :, cols]
            message(
                ("d", color, dy), "d", NZ * ROWS * spans[color][1] * 2,
                lambda piece=piece: [(piece(0), piece(1), at_e(0, 1))],
            )
            needs = sum((filled[(color, dy, dz)] for dz in range(NZ)), [])
            tasks[("share", color, dy)] = Task(needs, [("d", color, dy)], after=["start"], rank=2)

    gr = g_ref.shape[0] // 2
    gk = g_ref.shape[1]

    def g_parts():
        for k in range(NE):
            for o in range(2):
                if (k, o) != (0, 0):
                    rows = pl.multiple_of(lax.rem(c + o, 2) * gr, gr)
                    yield (
                        g_ref.at[pl.ds(rows, gr), :],
                        gbuf.at[pl.ds(pl.multiple_of(e * gr, gr), gr), pl.ds(o * gk, gk)],
                        at_e(k, o),
                    )

    message("g", "x", 15 * gr * gk, lambda: list(g_parts()), gbuf.at[pl.ds(0, 15 * gr // 2), :])
    message("bo", "d", gk * outs * 2, lambda: [(bo_ref, bobuf.at[pl.ds(gk, gk), :], at_e(0, 1))])

    half_outs = outs // 2
    for sign in (1, -1):
        for s in range(NY // 2):
            slot = ring.at[0 if sign > 0 else 1, s]
            if s == 0:
                cols = pl.ds(0 if sign > 0 else half_outs, half_outs)
                src = pp.at[lax.rem(y + NY // 2, NY), :, cols]
                parts = lambda src=src, dst=slot.at[:, cols], sign=sign: [(src, dst, at_y(sign))]
            else:
                src = ring.at[0 if sign > 0 else 1, s - 1]
                parts = lambda src=src, dst=slot, sign=sign: [(src, dst, at_y(sign))]
            message(("p", sign, s), "y+" if sign > 0 else "y-", gr * outs * (2 if s == 0 else 4), parts)

    def project_out():
        total = jnp.dot(gbuf[...], bobuf[...], preferred_element_type=F32)
        pp[...] = total.reshape(pp.shape)

    tasks["p0"] = Task(["g", "bo"], [("p", 1, 0), ("p", -1, 0)], project_out, 0.8, ["start"])
    for sign in (1, -1):
        for s in range(1, NY // 2):

            def add(sign=sign, s=s):
                index = 0 if sign > 0 else 1
                own = pp.at[lax.rem(y + sign * (NY // 2 - s) + NY, NY)]
                if s == 1:
                    near = pl.ds(0 if sign > 0 else half_outs, half_outs)
                    far = pl.ds(half_outs if sign > 0 else 0, half_outs)
                    ring[index, s - 1, :, near] = ring[index, s - 1, :, near] + own[:, near]
                    ring[index, s - 1, :, far] = own[:, far]
                else:
                    ring[index, s - 1] = ring[index, s - 1] + own[...]

            tasks[("padd", sign, s)] = Task([("p", sign, s - 1)], [("p", sign, s)], add, 0.15, ["p0"])

    def sum_y():
        zown[...] = (pp[y] + ring[0, NY // 2 - 1] + ring[1, NY // 2 - 1]).reshape(zown.shape)

    message(
        "pz", "z+", 4 * ROWS * outs * 4,
        lambda: [(zown.at[lax.rem(zh + k, NZ)], zbuf.at[k - 1], at_z(k)) for k in range(1, NZ)],
        zbuf,
    )
    tasks["psum"] = Task([("p", 1, NY // 2 - 1), ("p", -1, NY // 2 - 1)], ["pz"], sum_y, 0.2, ["p0"])

    def finish_p():
        total = zown[zh] + zbuf[0] + zbuf[1] + zbuf[2]
        pall_ref[y, c, zh] = total.astype(BF)

    message(
        "pgz", "z+", 4 * ROWS * outs * 2,
        lambda: [(pall_ref.at[y, c, zh], pall_ref.at[y, c, zh], at_z(k)) for k in range(1, NZ)],
        pall_ref.at[0, 0, pl.ds(0, NZ - 1)],
    )
    tasks["pfin"] = Task(["pz"], ["pgz"], finish_p, 0.1, ["psum"])
    for sign in (1, -1):
        for s in range(NY // 2):
            rows = pl.ds(0, NZ) if s < NY // 2 - 1 else pl.ds(0 if sign > 0 else NZ // 2, NZ // 2)
            place = pall_ref.at[lax.rem(y - sign * s + NY, NY), c, rows]
            message(
                ("pg", sign, s), "y+" if sign > 0 else "y-", gr * outs * 2 // (1 if s < NY // 2 - 1 else 2),
                lambda place=place, sign=sign: [(place, place, at_y(sign))],
            )
    for off in range(NY):
        place = pall_ref.at[lax.rem(y + off, NY), c]
        message(("pd", off), "d", gr * outs * 2, lambda place=place: [(place, place, at_e(0, 1))])
    tasks[("pgo", 0)] = Task(["pgz"], [("pg", 1, 0), ("pg", -1, 0), ("pd", 0)], after=["pfin"])
    for s in range(1, NY // 2):
        for sign in (1, -1):
            tasks[("pgo", s, sign)] = Task(
                [("pg", sign, s - 1)], [("pg", sign, s), ("pd", (-sign * s) % NY)], after=["pfin"]
            )
    far = NY // 2
    tasks[("pgo", far)] = Task([("pg", 1, far - 1), ("pg", -1, far - 1)], [("pd", far)], after=["pfin"])

    def own_place(dy):
        core = lax.rem(c + e // NZ, 2)
        return lax.rem(zh + lax.rem(e, NZ), NZ) * (NY * 2) + lax.rem(y + dy, NY) * 2 + core

    tile = 512
    for dy in range(NY):

        def project_in(dy=dy):
            part[...] = jnp.zeros_like(part)

            @pl.loop(0, feats // tile)
            def _(t):
                cols = pl.ds(pl.multiple_of(t * tile, tile), tile)
                rows = abuf[dy, :, :, :, cols].reshape(2 * NZ * ROWS, tile)
                part[...] += jnp.dot(rows, bbuf[cols, :], preferred_element_type=F32)

            mine[dy] = part[pl.ds(pl.multiple_of(e * ROWS, ROWS), ROWS), :]
            rsend[dy] = part[...].reshape(NE, ROWS, width).astype(BF)

        def sum_in(dy=dy):
            total = mine[dy]
            for k in range(NE - 1):
                total = total + rbuf[dy, k].astype(F32)
            pi_ref[own_place(dy)] = total.astype(BF)

        message(
            ("rs", dy), "x", 8 * ROWS * width,
            lambda dy=dy: [
                (rsend.at[dy, lax.rem(e + k, NE)], rbuf.at[dy, k - 1], at_e(k)) for k in range(1, NE)
            ],
            rbuf.at[dy],
        )
        message(
            ("ag", dy), "x", 8 * ROWS * width,
            lambda dy=dy: [
                (pi_ref.at[own_place(dy)], pi_ref.at[own_place(dy)], at_e(k)) for k in range(1, NE)
            ],
            pi_ref.at[pl.ds(0, NE - 1)],
        )
        shared = [("share", color, dy) for color in range(2)]
        tasks[("mm", dy)] = Task(
            [("d", 0, dy), ("d", 1, dy)], [("rs", dy)], project_in, 1.0, ["start", *shared], rank=3
        )
        tasks[("sum", dy)] = Task([("rs", dy)], [("ag", dy)], sum_in, 0.2, [("mm", dy)], rank=2)

    def begin():
        abuf[0, 0, 0] = a_ref[...]
        gbuf[pl.ds(pl.multiple_of(e * gr, gr), gr), pl.ds(0, gk)] = g_ref[pl.ds(pl.multiple_of(c * gr, gr), gr), :]
        bobuf[pl.ds(0, gk), :] = bo_ref[...]

    tasks["start"] = Task([], ["g", "bo", *own_sends], begin, 0.3)
    for name, task in tasks.items():
        if name != "start" and not task.needs and not task.after:
            task.after = ["start"]

    waited = set()
    started = []

    def wait_for(name):
        if name in waited:
            return
        waited.add(name)
        item = messages[name]
        if item.whole is None:
            item.copies[0].wait_recv()
        else:
            ref, index = item.whole
            pltpu.make_async_copy(ref, ref, rsem.at[index]).wait()

    loaded = False
    for name in ordered(tasks, messages):
        task = tasks[name]
        for m in task.needs:
            wait_for(m)
        if name == "start":
            for m in task.sends:
                item = messages[m]
                item.copies = item.make()
                for copy in item.copies:
                    copy.start()
                started.append(item)
            task.run()
            continue
        if name[0] == "mm" and not loaded:
            load_b.wait()
            loaded = True
        if task.run is not None:
            task.run()
        for m in task.sends:
            item = messages[m]
            item.copies = item.make()
            for copy in item.copies:
                copy.start()
            started.append(item)
    for name in messages:
        wait_for(name)
    for item in started:
        for copy in item.copies:
            copy.wait_send()


def combine(ids_ref, pout_ref, pin_ref, out_ref):
    tokens = pin_ref.shape[0]
    examples = NE
    window = MOST + ROWS
    ids = ids_ref[...]
    bounds = [jnp.sum((ids < n).astype(jnp.int32)) for n in range(examples + 1)]
    for n in range(examples):
        begin, end = bounds[n], bounds[n + 1]
        start = jnp.minimum((begin // ROWS) * ROWS, tokens - window)
        start = pl.multiple_of(start, ROWS)
        place = start + lax.broadcasted_iota(jnp.int32, (window, 1), 0)
        keep = (place >= begin) & (place < end)
        left = jnp.where(keep, pout_ref[pl.ds(start, window), :], 0)
        grad = lax.dot_general(
            left, pin_ref[pl.ds(start, window), :], (((0,), (0,)), ((), ())), preferred_element_type=F32
        )
        if n == 0:
            out_ref[...] = grad * grad
        elif n < examples - 1:
            out_ref[...] += grad * grad
        else:
            out_ref[...] = (out_ref[...] + grad * grad) * (1.0 / examples)


def local(activations, out_grads, basis_in, basis_out, example_ids):
    feats, width = basis_in.shape
    outs = basis_out.shape[1]
    tokens = example_ids.shape[0]
    gk = out_grads.shape[1]
    gr = out_grads.shape[0] // 2
    vmem = pl.BlockSpec(memory_space=pltpu.VMEM)
    wide1 = (feats * 22 // 28) // 256 * 256
    proj_in, proj_out = pl.pallas_call(
        functools.partial(exchange, wide1),
        out_shape=(
            jax.ShapeDtypeStruct((tokens // ROWS, ROWS, width), BF),
            jax.ShapeDtypeStruct((NY, 2, NZ, ROWS, outs), BF),
        ),
        in_specs=[vmem, vmem, pl.BlockSpec(memory_space=pl.ANY), vmem],
        out_specs=(vmem, vmem),
        scratch_shapes=[
            pltpu.VMEM((NY, 2, NZ, ROWS, feats), BF),
            pltpu.VMEM((feats, width), BF),
            pltpu.VMEM((NE * gr, 2 * gk), BF),
            pltpu.VMEM((2 * gk, outs), BF),
            pltpu.VMEM((NY, gr, outs), F32),
            pltpu.VMEM((2, NY // 2, gr, outs), F32),
            pltpu.VMEM((NZ, ROWS, outs), F32),
            pltpu.VMEM((NZ - 1, ROWS, outs), F32),
            pltpu.VMEM((2 * NZ * ROWS, width), F32),
            pltpu.VMEM((NY, ROWS, width), F32),
            pltpu.VMEM((NY, NE, ROWS, width), BF),
            pltpu.VMEM((NY, NE - 1, ROWS, width), BF),
            pltpu.SemaphoreType.DMA((256,)),
            pltpu.SemaphoreType.DMA((160,)),
            pltpu.SemaphoreType.DMA((1,)),
        ],
        compiler_params=pltpu.CompilerParams(
            collective_id=0, has_side_effects=True, vmem_limit_bytes=48 << 20
        ),
        name="exchange",
    )(activations, out_grads, basis_in, basis_out)
    return pl.pallas_call(
        combine,
        out_shape=jax.ShapeDtypeStruct((outs, width), F32),
        in_specs=[vmem] * 3,
        out_specs=vmem,
        compiler_params=pltpu.CompilerParams(vmem_limit_bytes=48 << 20),
        name="combine",
    )(example_ids.reshape(-1, 128), proj_out.reshape(tokens, outs), proj_in.reshape(tokens, width))


def solution(mesh):
    finer = Mesh(mesh.devices.reshape(2, NX, NZ, NY, 2), AXES)
    placed = (P(BLK, EX), P(EX, BLK), P(EX, BLK), P(BLK, EX), P())
    return jax.shard_map(local, mesh=finer, in_specs=placed, out_specs=P(EX, BLK), check_vma=False)
```

```python
import functools

import jax
import jax.numpy as jnp
from jax import lax
from jax.experimental import pallas as pl
from jax.experimental.pallas import tpu as pltpu
from jax.sharding import Mesh
from jax.sharding import PartitionSpec as P

AXES = ("zl", "x", "zh", "y", "c")
EX = ("zl", "x")
BLK = ("zh", "y", "c")
MESH = pl.DeviceIdType.MESH
MOST = 192
NX, NY, NZ, NE = 4, 8, 4, 8
ROWS = 16
BF = jnp.bfloat16
F32 = jnp.float32

RATE = {"y+": 40e3, "y-": 40e3, "z+": 16e3, "z-": 16e3, "x": 46e3, "d": 600e3}
LAG = {"y+": 3.0, "y-": 3.0, "z+": 4.0, "z-": 4.0, "x": 5.0, "d": 2.0}
BACKLOG = 1.0


class Message:
    def __init__(self, link, nbytes, make, whole, rank):
        self.link, self.nbytes, self.make, self.whole, self.rank = link, nbytes, make, whole, rank
        self.copies = None


class Task:
    def __init__(self, needs, sends, run=None, cost=0.05, after=(), rank=0):
        self.needs, self.sends, self.run = needs, sends, run
        self.cost, self.after, self.rank = cost, after, rank


def ordered(tasks, messages):
    free = dict.fromkeys(RATE, 0.0)
    arrived, done, now, order = {}, {}, 0.0, []
    left, pending = dict(tasks), []
    while left or pending:
        moments = []
        for number, (rank, m) in enumerate(pending):
            when = free[messages[m].link] - BACKLOG
            moments.append((max(when, now), 0, rank, number, m))
        for number, (name, task) in enumerate(left.items()):
            if any(m not in arrived for m in task.needs) or any(t not in done for t in task.after):
                continue
            ready = max([arrived[m] for m in task.needs] + [done[t] for t in task.after] + [0.0])
            moments.append((max(ready, now), 1, (task.rank, ready), number, name))
        now, is_task, key, _, name = min(moments, key=lambda moment: moment[:4])
        if is_task:
            task = left.pop(name)
            now += task.cost
            done[name] = now
            pending += [(messages[m].rank, m) for m in task.sends]
        else:
            pending.remove((key, name))
            message = messages[name]
            free[message.link] = max(now, free[message.link]) + message.nbytes / RATE[message.link]
            arrived[name] = free[message.link] + LAG[message.link]
            now += 0.03
        order.append((is_task, name))
    return order


def exchange(
    wide1,
    a_ref, g_ref, b_hbm, bo_ref, ids_ref, out_ref,
    pi_ref, pall_ref, abuf, bbuf, gbuf, bobuf, pp, ring, zown, zbuf, part, mine, rsend, rbuf,
    ssem, rsem, bsem,
):
    zl, x, zh, y, c = (lax.axis_index(n) for n in AXES)
    e = zl * NX + x
    feats = a_ref.shape[1]
    outs = bo_ref.shape[1]
    width = b_hbm.shape[0]
    spans = ((0, wide1), (wide1, feats - wide1))

    def at_y(d):
        return (zl, x, zh, lax.rem(y + d + NY, NY), c)

    def at_z(d):
        return (zl, x, lax.rem(zh + d + NZ, NZ), y, c)

    def at_e(k, other=0):
        ek = lax.rem(e + k, NE)
        return (ek // NX, lax.rem(ek, NX), zh, y, lax.rem(c + other, 2))

    load_b = pltpu.make_async_copy(b_hbm, bbuf, bsem.at[0])
    load_b.start()

    partners = [at_y(1), at_y(-1), at_z(1), at_z(2), at_z(3)]
    partners += [at_e(k, o) for k in range(NE) for o in range(2) if (k, o) != (0, 0)]
    barrier = pltpu.get_barrier_semaphore()
    for device in partners:
        pl.semaphore_signal(barrier, inc=1, device_id=device, device_id_type=MESH)
    pl.semaphore_wait(barrier, len(partners))

    messages, tasks = {}, {}
    counts = [0, 0]

    def message(name, link, nbytes, parts, whole=None, rank=1):
        arrival = counts[1]
        counts[1] += 1

        def make():
            copies = []
            for src, dst, device in parts():
                copies.append(
                    pltpu.make_async_remote_copy(
                        src_ref=src, dst_ref=dst,
                        send_sem=ssem.at[counts[0]], recv_sem=rsem.at[arrival],
                        device_id=device, device_id_type=MESH,
                    )
                )
                counts[0] += 1
            return copies

        rank = 0 if name[0] in "pg" else rank
        messages[name] = Message(link, nbytes, make, None if whole is None else (whole, arrival), rank)

    def a_slot(color, dy, dz, half=None, own=True):
        at, size = spans[color]
        if half is not None:
            size //= 2
            at += half * size
        cols = pl.ds(at, size)
        if own and (dy, dz) == (0, 0):
            return a_ref.at[:, cols], size
        return abuf.at[dy, 0, dz, :, cols], size

    def a_message(color, dy, dz, axis, sign, half=None):
        sy, sz = ((dy + sign) % NY, dz) if axis == "y" else (dy, (dz + sign) % NZ)
        size = a_slot(color, dy, dz, half)[1]
        device = at_y(sign) if axis == "y" else at_z(sign)
        name = ("a", color, dy, dz, half)
        message(
            name, axis + ("+" if sign > 0 else "-"), ROWS * size * 2,
            lambda: [(a_slot(color, sy, sz, half)[0], a_slot(color, dy, dz, half, False)[0], device)],
        )
        return name

    def along(color, axis, count, fixed):
        steps = {}
        for sign in (1, -1):
            chain = []
            for d in range(1, count // 2 + 1):
                place = (-sign * d) % count
                half = None if d < count // 2 else (0 if sign > 0 else 1)
                dy, dz = (place, fixed) if axis == "y" else (fixed, place)
                chain.append((a_message(color, dy, dz, axis, sign, half), (dy, dz)))
            steps[sign] = chain
        return steps

    first_sends = []
    filled = {(0, 0, 0): [], (1, 0, 0): []}
    starts = {}

    def ring_tasks(color, axis, fixed, from_task, rank):
        steps = along(color, axis, NY if axis == "y" else NZ, fixed)
        for sign in (1, -1):
            chain = steps[sign]
            for (name, place), (following, _) in zip(chain, chain[1:]):
                tasks[("fwd", name)] = Task([name], [following], rank=rank)
            for name, place in chain:
                filled.setdefault((color, *place), []).append(name)
        return [steps[1][0][0], steps[-1][0][0]]

    if True:
        own_sends = []
        own_sends += ring_tasks(0, "z", 0, None, 0)
        for dz in (0, 1, 3, 2):
            sends = ring_tasks(0, "y", dz, None, 1)
            if dz == 0:
                own_sends += sends
            else:
                starts[(0, 0, dz)] = sends
        sends = ring_tasks(1, "y", 0, None, 0)
        own_sends += sends
        for dy in (0, 1, 7, 2, 6, 3, 5, 4):
            sends = ring_tasks(1, "z", dy, None, 1)
            if dy == 0:
                own_sends += sends
            else:
                starts[(1, dy, 0)] = sends
        for place, sends in starts.items():
            tasks[("go", place)] = Task(filled[place], sends, rank=1)

    for dy in range(NY):
        for color in range(2):
            cols = pl.ds(*spans[color])
            piece = lambda slot, dy=dy, cols=cols: abuf.at[dy, slot, :, :, cols]
            message(
                ("d", color, dy), "d", NZ * ROWS * spans[color][1] * 2,
                lambda piece=piece: [(piece(0), piece(1), at_e(0, 1))],
            )
            needs = sum((filled[(color, dy, dz)] for dz in range(NZ)), [])
            tasks[("share", color, dy)] = Task(needs, [("d", color, dy)], after=["place"], rank=2)

    gr = g_ref.shape[0] // 2
    gk = g_ref.shape[1]

    def g_parts():
        for k in range(NE):
            for o in range(2):
                if (k, o) != (0, 0):
                    rows = pl.multiple_of(lax.rem(c + o, 2) * gr, gr)
                    yield (
                        g_ref.at[pl.ds(rows, gr), :],
                        gbuf.at[pl.ds(pl.multiple_of(e * gr, gr), gr), pl.ds(o * gk, gk)],
                        at_e(k, o),
                    )

    message("g", "x", 15 * gr * gk, lambda: list(g_parts()), gbuf.at[pl.ds(0, 15 * gr // 2), :])
    message("bo", "d", gk * outs * 2, lambda: [(bo_ref, bobuf.at[pl.ds(gk, gk), :], at_e(0, 1))])

    half_outs = outs // 2
    lanes = outs // 2
    p_starts = []
    for sign in (1, -1):
        side = 0 if sign > 0 else 1
        for lane in range(2):
            cols = pl.ds(lane * lanes, lanes)
            first = 0 if lane == side else 1
            for s in range(first, NY // 2):
                if s == first:
                    src = pp.at[lax.rem(y + sign * (NY // 2 - s) + NY, NY), :, cols]
                    p_starts.append(("p", sign, lane, s))
                else:
                    src = ring.at[side, s - 1, :, cols]
                message(
                    ("p", sign, lane, s), "y+" if sign > 0 else "y-", gr * lanes * 4,
                    lambda src=src, dst=ring.at[side, s, :, cols], sign=sign: [(src, dst, at_y(sign))],
                )

    def project_out():
        total = jnp.dot(gbuf[...], bobuf[...], preferred_element_type=F32)
        pp[...] = total.reshape(pp.shape)

    tasks["p0"] = Task(["g", "bo"], p_starts, project_out, 0.8, ["place"])
    for sign in (1, -1):
        side = 0 if sign > 0 else 1
        for lane in range(2):
            for s in range(1 if lane == side else 2, NY // 2):

                def add(sign=sign, side=side, cols=pl.ds(lane * lanes, lanes), s=s):
                    own = pp.at[lax.rem(y + sign * (NY // 2 - s) + NY, NY), :, cols]
                    ring[side, s - 1, :, cols] = ring[side, s - 1, :, cols] + own[...]

                tasks[("padd", sign, lane, s)] = Task(
                    [("p", sign, lane, s - 1)], [("p", sign, lane, s)], add, 0.1, ["p0"]
                )

    def sum_y():
        zown[...] = (pp[y] + ring[0, NY // 2 - 1] + ring[1, NY // 2 - 1]).reshape(zown.shape)

    message(
        "pz", "z+", 2 * ROWS * outs * 4,
        lambda: [(zown.at[lax.rem(zh + k, NZ)], zbuf.at[k - 1], at_z(k)) for k in range(1, NZ)],
        zbuf,
    )
    last = [("p", sign, lane, NY // 2 - 1) for sign in (1, -1) for lane in range(2)]
    tasks["psum"] = Task(last, ["pz"], sum_y, 0.2, ["p0"])

    def p_place(at):
        return at * (2 * NZ) + c * NZ

    def finish_p():
        total = zown[zh] + zbuf[0] + zbuf[1] + zbuf[2]
        pall_ref[p_place(y) + zh] = total.astype(BF)

    message(
        "pgz", "z+", 2 * ROWS * outs * 2,
        lambda: [(pall_ref.at[p_place(y) + zh], pall_ref.at[p_place(y) + zh], at_z(k)) for k in range(1, NZ)],
        pall_ref.at[pl.ds(0, NZ - 1)],
    )
    tasks["pfin"] = Task(["pz"], ["pgz"], finish_p, 0.1, ["psum"])
    piece = NZ // 2
    p_filled = {off: [] for off in range(NY)}
    p_goes = []
    for sign in (1, -1):
        side = 0 if sign > 0 else 1
        for lane in range(2):
            hops = NY // 2 if lane == side else NY // 2 - 1
            for s in range(hops):
                place = pall_ref.at[pl.ds(p_place(lax.rem(y - sign * s + NY, NY)) + lane * piece, piece)]
                name = ("pg", sign, lane, s)
                message(
                    name, "y+" if sign > 0 else "y-", piece * ROWS * outs * 2,
                    lambda place=place, sign=sign: [(place, place, at_y(sign))],
                )
                p_filled[(-sign * (s + 1)) % NY].append(name)
                if s == 0:
                    p_goes.append(name)
                else:
                    tasks[("pgo", sign, lane, s)] = Task([("pg", sign, lane, s - 1)], [name], after=["pfin"])
    for off in range(NY):
        place = pall_ref.at[pl.ds(p_place(lax.rem(y + off, NY)), NZ)]
        message(("pd", off), "d", gr * outs * 2, lambda place=place: [(place, place, at_e(0, 1))])
    tasks["pgo"] = Task(["pgz"], [*p_goes, ("pd", 0)], after=["pfin"])
    for off in range(1, NY):
        tasks[("pdo", off)] = Task(p_filled[off], [("pd", off)], after=["pfin"])

    def own_place(dy):
        core = lax.rem(c + e // NZ, 2)
        return lax.rem(zh + lax.rem(e, NZ), NZ) * (NY * 2) + lax.rem(y + dy, NY) * 2 + core

    tile = 512
    for dy in range(NY):

        def project_in(dy=dy):
            part[...] = jnp.zeros_like(part)

            @pl.loop(0, feats // tile)
            def _(t):
                cols = pl.ds(pl.multiple_of(t * tile, tile), tile)
                rows = abuf[dy, :, :, :, cols].reshape(2 * NZ * ROWS, tile)
                part[...] += lax.dot_general(
                    rows, bbuf[:, cols], (((1,), (1,)), ((), ())), preferred_element_type=F32
                )

            mine[dy] = part[pl.ds(pl.multiple_of(e * ROWS, ROWS), ROWS), :]
            rsend[dy] = part[...].reshape(NE, ROWS, width).astype(BF)

        def sum_in(dy=dy):
            total = mine[dy]
            for k in range(NE - 1):
                total = total + rbuf[dy, k].astype(F32)
            pi_ref[own_place(dy)] = total.astype(BF)

        message(
            ("rs", dy), "x", 8 * ROWS * width,
            lambda dy=dy: [
                (rsend.at[dy, lax.rem(e + k, NE)], rbuf.at[dy, k - 1], at_e(k)) for k in range(1, NE)
            ],
            rbuf.at[dy],
        )
        message(
            ("ag", dy), "x", 8 * ROWS * width,
            lambda dy=dy: [
                (pi_ref.at[own_place(dy)], pi_ref.at[own_place(dy)], at_e(k)) for k in range(1, NE)
            ],
            pi_ref.at[pl.ds(0, NE - 1)],
        )
        shared = [("share", color, dy) for color in range(2)]
        tasks[("mm", dy)] = Task(
            [("d", 0, dy), ("d", 1, dy)], [("rs", dy)], project_in, 1.0, ["place", *shared], rank=3
        )
        tasks[("sum", dy)] = Task([("rs", dy)], [("ag", dy)], sum_in, 0.2, [("mm", dy)], rank=2)

    def begin():
        abuf[0, 0, 0] = a_ref[...]
        gbuf[pl.ds(pl.multiple_of(e * gr, gr), gr), pl.ds(0, gk)] = g_ref[pl.ds(pl.multiple_of(c * gr, gr), gr), :]
        bobuf[pl.ds(0, gk), :] = bo_ref[...]

    tasks["start"] = Task([], ["g", "bo", *own_sends])
    tasks["place"] = Task([], [], begin, 0.3, ["start"], rank=-1)
    for name, task in tasks.items():
        if name != "start" and not task.needs and not task.after:
            task.after = ["start"]

    waited = set()
    started = []

    def wait_for(name):
        if name in waited:
            return
        waited.add(name)
        item = messages[name]
        if item.whole is None:
            item.copies[0].wait_recv()
        else:
            ref, index = item.whole
            pltpu.make_async_copy(ref, ref, rsem.at[index]).wait()

    loaded = False
    for is_task, name in ordered(tasks, messages):
        if not is_task:
            item = messages[name]
            item.copies = item.make()
            for copy in item.copies:
                copy.start()
            started.append(item)
            continue
        task = tasks[name]
        for m in task.needs:
            wait_for(m)
        if name[0] == "mm" and not loaded:
            load_b.wait()
            loaded = True
        if task.run is not None:
            task.run()
    for name in messages:
        wait_for(name)
    combine(ids_ref, pall_ref, pi_ref, out_ref)
    for item in started:
        for copy in item.copies:
            copy.wait_send()


def combine(ids_ref, pout_ref, pin_ref, out_ref):
    blocks = pin_ref.shape[0]
    window = MOST // ROWS + 1
    ids = ids_ref[...]
    bounds = [jnp.sum((ids < n).astype(jnp.int32)) for n in range(NE + 1)]
    for n in range(NE):
        begin, end = bounds[n], bounds[n + 1]
        start = jnp.minimum(begin // ROWS, blocks - window)
        place = start * ROWS + lax.broadcasted_iota(jnp.int32, (window * ROWS, 1), 0)
        keep = (place >= begin) & (place < end)
        left = pout_ref[pl.ds(start, window)].reshape(window * ROWS, -1)
        right = pin_ref[pl.ds(start, window)].reshape(window * ROWS, -1)
        grad = lax.dot_general(
            right, jnp.where(keep, left, 0), (((0,), (0,)), ((), ())), preferred_element_type=F32
        )
        if n == 0:
            out_ref[...] = grad * grad
        elif n < NE - 1:
            out_ref[...] += grad * grad
        else:
            out_ref[...] = (out_ref[...] + grad * grad) * (1.0 / NE)


def local(activations, out_grads, basis_in, basis_out, example_ids):
    feats, width = basis_in.shape
    outs = basis_out.shape[1]
    tokens = example_ids.shape[0]
    gk = out_grads.shape[1]
    gr = out_grads.shape[0] // 2
    vmem = pl.BlockSpec(memory_space=pltpu.VMEM)
    wide1 = (feats * 22 // 28) // 256 * 256
    correction = pl.pallas_call(
        functools.partial(exchange, wide1),
        out_shape=jax.ShapeDtypeStruct((width, outs), F32),
        in_specs=[vmem, vmem, pl.BlockSpec(memory_space=pl.ANY), vmem, vmem],
        out_specs=vmem,
        scratch_shapes=[
            pltpu.VMEM((tokens // ROWS, ROWS, width), BF),
            pltpu.VMEM((tokens // ROWS, ROWS, outs), BF),
            pltpu.VMEM((NY, 2, NZ, ROWS, feats), BF),
            pltpu.VMEM((width, feats), BF),
            pltpu.VMEM((NE * gr, 2 * gk), BF),
            pltpu.VMEM((2 * gk, outs), BF),
            pltpu.VMEM((NY, gr, outs), F32),
            pltpu.VMEM((2, NY // 2, gr, outs), F32),
            pltpu.VMEM((NZ, ROWS, outs), F32),
            pltpu.VMEM((NZ - 1, ROWS, outs), F32),
            pltpu.VMEM((2 * NZ * ROWS, width), F32),
            pltpu.VMEM((NY, ROWS, width), F32),
            pltpu.VMEM((NY, NE, ROWS, width), BF),
            pltpu.VMEM((NY, NE - 1, ROWS, width), BF),
            pltpu.SemaphoreType.DMA((320,)),
            pltpu.SemaphoreType.DMA((240,)),
            pltpu.SemaphoreType.DMA((1,)),
        ],
        compiler_params=pltpu.CompilerParams(
            collective_id=0, has_side_effects=True, vmem_limit_bytes=60 << 20
        ),
        name="exchange",
    )(activations, out_grads, basis_in.T, basis_out, example_ids.reshape(-1, 128))
    return correction.T


def solution(mesh):
    finer = Mesh(mesh.devices.reshape(2, NX, NZ, NY, 2), AXES)
    placed = (P(BLK, EX), P(EX, BLK), P(EX, BLK), P(BLK, EX), P())
    return jax.shard_map(local, mesh=finer, in_specs=placed, out_specs=P(EX, BLK), check_vma=False)
```

```python
import functools

import jax
import jax.numpy as jnp
from jax import lax
from jax.experimental import pallas as pl
from jax.experimental.pallas import tpu as pltpu
from jax.sharding import Mesh
from jax.sharding import PartitionSpec as P

AXES = ("zl", "x", "zh", "y", "c")
EX = ("zl", "x")
BLK = ("zh", "y", "c")
MESH = pl.DeviceIdType.MESH
MOST = 192
NX, NY, NZ, NE = 4, 8, 4, 8
ROWS = 16
BF = jnp.bfloat16
F32 = jnp.float32

RATE = {"y+": 36e3, "y-": 36e3, "z+": 16e3, "z-": 16e3, "x": 46e3, "d": 600e3}
LAG = {"y+": 3.0, "y-": 3.0, "z+": 4.0, "z-": 4.0, "x": 5.0, "d": 2.0}
BACKLOG = 1.0


class Message:
    def __init__(self, link, nbytes, make, whole, rank):
        self.link, self.nbytes, self.make, self.whole, self.rank = link, nbytes, make, whole, rank
        self.copies = None


class Task:
    def __init__(self, needs, sends, run=None, cost=0.05, after=(), rank=0):
        self.needs, self.sends, self.run = needs, sends, run
        self.cost, self.after, self.rank = cost, after, rank


def ordered(tasks, messages):
    free = dict.fromkeys(RATE, 0.0)
    arrived, done, now, order = {}, {}, 0.0, []
    left, pending = dict(tasks), []
    while left or pending:
        moments = []
        for number, (rank, m) in enumerate(pending):
            when = free[messages[m].link] - BACKLOG
            moments.append((max(when, now), 0, rank, number, m))
        for number, (name, task) in enumerate(left.items()):
            if any(m not in arrived for m in task.needs) or any(t not in done for t in task.after):
                continue
            ready = max([arrived[m] for m in task.needs] + [done[t] for t in task.after] + [0.0])
            moments.append((max(ready, now), 1, (task.rank, ready), number, name))
        now, is_task, key, _, name = min(moments, key=lambda moment: moment[:4])
        if is_task:
            task = left.pop(name)
            now += task.cost
            done[name] = now
            pending += [(messages[m].rank, m) for m in task.sends]
        else:
            pending.remove((key, name))
            message = messages[name]
            free[message.link] = max(now, free[message.link]) + message.nbytes / RATE[message.link]
            arrived[name] = free[message.link] + LAG[message.link]
            now += 0.03
        order.append((is_task, name))
    return order


def exchange(
    wide1,
    a_ref, g_ref, b_hbm, bo_ref, ids_ref, out_ref,
    pi_ref, pall_ref, abuf, bbuf, gbuf, bobuf, pp, ring, zown, zbuf, part, mine, rsend, rbuf,
    ssem, rsem, bsem,
):
    zl, x, zh, y, c = (lax.axis_index(n) for n in AXES)
    e = zl * NX + x
    feats = a_ref.shape[1]
    outs = bo_ref.shape[1]
    width = b_hbm.shape[0]
    spans = ((0, wide1), (wide1, feats - wide1))

    def at_y(d):
        return (zl, x, zh, lax.rem(y + d + NY, NY), c)

    def at_z(d):
        return (zl, x, lax.rem(zh + d + NZ, NZ), y, c)

    def at_e(k, other=0):
        ek = lax.rem(e + k, NE)
        return (ek // NX, lax.rem(ek, NX), zh, y, lax.rem(c + other, 2))

    load_b = pltpu.make_async_copy(b_hbm, bbuf, bsem.at[0])
    load_b.start()

    partners = [at_y(1), at_y(-1), at_z(1), at_z(2), at_z(3)]
    partners += [at_e(k, o) for k in range(NE) for o in range(2) if (k, o) != (0, 0)]
    barrier = pltpu.get_barrier_semaphore()
    for device in partners:
        pl.semaphore_signal(barrier, inc=1, device_id=device, device_id_type=MESH)
    pl.semaphore_wait(barrier, len(partners))

    messages, tasks = {}, {}
    counts = [0, 0]

    def message(name, link, nbytes, parts, whole=None, rank=1):
        arrival = counts[1]
        counts[1] += 1

        def make():
            copies = []
            for src, dst, device in parts():
                copies.append(
                    pltpu.make_async_remote_copy(
                        src_ref=src, dst_ref=dst,
                        send_sem=ssem.at[counts[0]], recv_sem=rsem.at[arrival],
                        device_id=device, device_id_type=MESH,
                    )
                )
                counts[0] += 1
            return copies

        rank = 0 if name[0] in "pg" else rank
        messages[name] = Message(link, nbytes, make, None if whole is None else (whole, arrival), rank)

    def a_slot(color, dy, dz, half=None, own=True):
        at, size = spans[color]
        if half is not None:
            size //= 2
            at += half * size
        cols = pl.ds(at, size)
        if own and (dy, dz) == (0, 0):
            return a_ref.at[:, cols], size
        return abuf.at[dy, 0, dz, :, cols], size

    def a_message(color, dy, dz, axis, sign, half=None):
        sy, sz = ((dy + sign) % NY, dz) if axis == "y" else (dy, (dz + sign) % NZ)
        size = a_slot(color, dy, dz, half)[1]
        device = at_y(sign) if axis == "y" else at_z(sign)
        name = ("a", color, dy, dz, half)
        message(
            name, axis + ("+" if sign > 0 else "-"), ROWS * size * 2,
            lambda: [(a_slot(color, sy, sz, half)[0], a_slot(color, dy, dz, half, False)[0], device)],
        )
        return name

    def along(color, axis, count, fixed):
        steps = {}
        for sign in (1, -1):
            chain = []
            for d in range(1, count // 2 + 1):
                place = (-sign * d) % count
                half = None if d < count // 2 else (0 if sign > 0 else 1)
                dy, dz = (place, fixed) if axis == "y" else (fixed, place)
                chain.append((a_message(color, dy, dz, axis, sign, half), (dy, dz)))
            steps[sign] = chain
        return steps

    first_sends = []
    filled = {(0, 0, 0): [], (1, 0, 0): []}
    starts = {}

    def ring_tasks(color, axis, fixed, from_task, rank):
        steps = along(color, axis, NY if axis == "y" else NZ, fixed)
        for sign in (1, -1):
            chain = steps[sign]
            for (name, place), (following, _) in zip(chain, chain[1:]):
                tasks[("fwd", name)] = Task([name], [following], rank=rank)
            for name, place in chain:
                filled.setdefault((color, *place), []).append(name)
        return [steps[1][0][0], steps[-1][0][0]]

    if True:
        own_sends = []
        own_sends += ring_tasks(0, "z", 0, None, 0)
        for dz in (0, 1, 3, 2):
            sends = ring_tasks(0, "y", dz, None, 1)
            if dz == 0:
                own_sends += sends
            else:
                starts[(0, 0, dz)] = sends
        sends = ring_tasks(1, "y", 0, None, 0)
        own_sends += sends
        for dy in (0, 1, 7, 2, 6, 3, 5, 4):
            sends = ring_tasks(1, "z", dy, None, 1)
            if dy == 0:
                own_sends += sends
            else:
                starts[(1, dy, 0)] = sends
        for place, sends in starts.items():
            tasks[("go", place)] = Task(filled[place], sends, rank=1)

    for dy in range(NY):
        for color in range(2):
            cols = pl.ds(*spans[color])
            piece = lambda slot, dy=dy, cols=cols: abuf.at[dy, slot, :, :, cols]
            message(
                ("d", color, dy), "d", NZ * ROWS * spans[color][1] * 2,
                lambda piece=piece: [(piece(0), piece(1), at_e(0, 1))],
            )
            needs = sum((filled[(color, dy, dz)] for dz in range(NZ)), [])
            tasks[("share", color, dy)] = Task(needs, [("d", color, dy)], after=["place"], rank=2)

    gr = g_ref.shape[0] // 2
    gk = g_ref.shape[1]

    def g_parts():
        for k in range(NE):
            for o in range(2):
                if (k, o) != (0, 0):
                    rows = pl.multiple_of(lax.rem(c + o, 2) * gr, gr)
                    yield (
                        g_ref.at[pl.ds(rows, gr), :],
                        gbuf.at[pl.ds(pl.multiple_of(e * gr, gr), gr), pl.ds(o * gk, gk)],
                        at_e(k, o),
                    )

    message("g", "x", 15 * gr * gk, lambda: list(g_parts()), gbuf.at[pl.ds(0, 15 * gr // 2), :])
    message("bo", "d", gk * outs * 2, lambda: [(bo_ref, bobuf.at[pl.ds(gk, gk), :], at_e(0, 1))])

    half_outs = outs // 2
    lanes = outs // 2
    p_starts = []
    for sign in (1, -1):
        side = 0 if sign > 0 else 1
        for lane in range(2):
            cols = pl.ds(lane * lanes, lanes)
            first = 0 if lane == side else 1
            for s in range(first, NY // 2):
                if s == first:
                    src = pp.at[lax.rem(y + sign * (NY // 2 - s) + NY, NY), :, cols]
                    p_starts.append(("p", sign, lane, s))
                else:
                    src = ring.at[side, s - 1, :, cols]
                message(
                    ("p", sign, lane, s), "y+" if sign > 0 else "y-", gr * lanes * 4,
                    lambda src=src, dst=ring.at[side, s, :, cols], sign=sign: [(src, dst, at_y(sign))],
                )

    def project_out():
        total = jnp.dot(gbuf[...], bobuf[...], preferred_element_type=F32)
        pp[...] = total.reshape(pp.shape)

    tasks["p0"] = Task(["g", "bo"], p_starts, project_out, 0.8, ["place"])
    for sign in (1, -1):
        side = 0 if sign > 0 else 1
        for lane in range(2):
            for s in range(1 if lane == side else 2, NY // 2):

                def add(sign=sign, side=side, cols=pl.ds(lane * lanes, lanes), s=s):
                    own = pp.at[lax.rem(y + sign * (NY // 2 - s) + NY, NY), :, cols]
                    ring[side, s - 1, :, cols] = ring[side, s - 1, :, cols] + own[...]

                tasks[("padd", sign, lane, s)] = Task(
                    [("p", sign, lane, s - 1)], [("p", sign, lane, s)], add, 0.1, ["p0"]
                )

    def sum_y():
        zown[...] = (pp[y] + ring[0, NY // 2 - 1] + ring[1, NY // 2 - 1]).reshape(zown.shape)

    message(
        "pz", "z+", 2 * ROWS * outs * 4,
        lambda: [(zown.at[lax.rem(zh + k, NZ)], zbuf.at[k - 1], at_z(k)) for k in range(1, NZ)],
        zbuf,
    )
    last = [("p", sign, lane, NY // 2 - 1) for sign in (1, -1) for lane in range(2)]
    tasks["psum"] = Task(last, ["pz"], sum_y, 0.2, ["p0"])

    def p_place(at):
        return at * (2 * NZ) + c * NZ

    def finish_p():
        total = zown[zh] + zbuf[0] + zbuf[1] + zbuf[2]
        pall_ref[p_place(y) + zh] = total.astype(BF)

    message(
        "pgz", "z+", 2 * ROWS * outs * 2,
        lambda: [(pall_ref.at[p_place(y) + zh], pall_ref.at[p_place(y) + zh], at_z(k)) for k in range(1, NZ)],
        pall_ref.at[pl.ds(0, NZ - 1)],
    )
    tasks["pfin"] = Task(["pz"], ["pgz"], finish_p, 0.1, ["psum"])
    piece = NZ // 2
    p_filled = {off: [] for off in range(NY)}
    p_goes = []
    for sign in (1, -1):
        side = 0 if sign > 0 else 1
        for lane in range(2):
            hops = NY // 2 if lane == side else NY // 2 - 1
            for s in range(hops):
                place = pall_ref.at[pl.ds(p_place(lax.rem(y - sign * s + NY, NY)) + lane * piece, piece)]
                name = ("pg", sign, lane, s)
                message(
                    name, "y+" if sign > 0 else "y-", piece * ROWS * outs * 2,
                    lambda place=place, sign=sign: [(place, place, at_y(sign))],
                )
                p_filled[(-sign * (s + 1)) % NY].append(name)
                if s == 0:
                    p_goes.append(name)
                else:
                    tasks[("pgo", sign, lane, s)] = Task([("pg", sign, lane, s - 1)], [name], after=["pfin"])
    for off in range(NY):
        place = pall_ref.at[pl.ds(p_place(lax.rem(y + off, NY)), NZ)]
        message(("pd", off), "d", gr * outs * 2, lambda place=place: [(place, place, at_e(0, 1))])
    tasks["pgo"] = Task(["pgz"], [*p_goes, ("pd", 0)], after=["pfin"])
    for off in range(1, NY):
        tasks[("pdo", off)] = Task(p_filled[off], [("pd", off)], after=["pfin"])

    def own_place(dy):
        core = lax.rem(c + e // NZ, 2)
        return lax.rem(zh + lax.rem(e, NZ), NZ) * (NY * 2) + lax.rem(y + dy, NY) * 2 + core

    tile = 512
    for dy in range(NY):

        def project_in(dy=dy):
            part[...] = jnp.zeros_like(part)

            @pl.loop(0, feats // tile)
            def _(t):
                cols = pl.ds(pl.multiple_of(t * tile, tile), tile)
                rows = abuf[dy, :, :, :, cols].reshape(2 * NZ * ROWS, tile)
                part[...] += lax.dot_general(
                    rows, bbuf[:, cols], (((1,), (1,)), ((), ())), preferred_element_type=F32
                )

            mine[dy] = part[pl.ds(pl.multiple_of(e * ROWS, ROWS), ROWS), :]
            rsend[dy] = part[...].reshape(NE, ROWS, width).astype(BF)

        def sum_in(dy=dy):
            total = mine[dy]
            for k in range(NE - 1):
                total = total + rbuf[dy, k].astype(F32)
            pi_ref[own_place(dy)] = total.astype(BF)

        message(
            ("rs", dy), "x", 8 * ROWS * width,
            lambda dy=dy: [
                (rsend.at[dy, lax.rem(e + k, NE)], rbuf.at[dy, k - 1], at_e(k)) for k in range(1, NE)
            ],
            rbuf.at[dy],
        )
        message(
            ("ag", dy), "x", 8 * ROWS * width,
            lambda dy=dy: [
                (pi_ref.at[own_place(dy)], pi_ref.at[own_place(dy)], at_e(k)) for k in range(1, NE)
            ],
            pi_ref.at[pl.ds(0, NE - 1)],
        )
        shared = [("share", color, dy) for color in range(2)]
        tasks[("mm", dy)] = Task(
            [("d", 0, dy), ("d", 1, dy)], [("rs", dy)], project_in, 1.0, ["place", *shared], rank=3
        )
        tasks[("sum", dy)] = Task([("rs", dy)], [("ag", dy)], sum_in, 0.2, [("mm", dy)], rank=2)

    def begin():
        abuf[0, 0, 0] = a_ref[...]
        gbuf[pl.ds(pl.multiple_of(e * gr, gr), gr), pl.ds(0, gk)] = g_ref[pl.ds(pl.multiple_of(c * gr, gr), gr), :]
        bobuf[pl.ds(0, gk), :] = bo_ref[...]

    tasks["start"] = Task([], ["g", "bo", *own_sends])
    tasks["place"] = Task([], [], begin, 0.3, ["start"], rank=-1)
    for name, task in tasks.items():
        if name != "start" and not task.needs and not task.after:
            task.after = ["start"]

    waited = set()
    started = []

    def wait_for(name):
        if name in waited:
            return
        waited.add(name)
        item = messages[name]
        if item.whole is None:
            item.copies[0].wait_recv()
        else:
            ref, index = item.whole
            pltpu.make_async_copy(ref, ref, rsem.at[index]).wait()

    loaded = False
    for is_task, name in ordered(tasks, messages):
        if not is_task:
            item = messages[name]
            item.copies = item.make()
            for copy in item.copies:
                copy.start()
            started.append(item)
            continue
        task = tasks[name]
        for m in task.needs:
            wait_for(m)
        if name[0] == "mm" and not loaded:
            load_b.wait()
            loaded = True
        if task.run is not None:
            task.run()
    for name in messages:
        wait_for(name)
    combine(ids_ref, pall_ref, pi_ref, out_ref)
    for item in started:
        for copy in item.copies:
            copy.wait_send()


def combine(ids_ref, pout_ref, pin_ref, out_ref):
    blocks = pin_ref.shape[0]
    window = MOST // ROWS + 1
    ids = ids_ref[...]
    bounds = [jnp.sum((ids < n).astype(jnp.int32)) for n in range(NE + 1)]
    for n in range(NE):
        begin, end = bounds[n], bounds[n + 1]
        start = jnp.minimum(begin // ROWS, blocks - window)
        place = start * ROWS + lax.broadcasted_iota(jnp.int32, (window * ROWS, 1), 0)
        keep = (place >= begin) & (place < end)
        left = pout_ref[pl.ds(start, window)].reshape(window * ROWS, -1)
        right = pin_ref[pl.ds(start, window)].reshape(window * ROWS, -1)
        grad = lax.dot_general(
            right, jnp.where(keep, left, 0), (((0,), (0,)), ((), ())), preferred_element_type=F32
        )
        if n == 0:
            out_ref[...] = grad * grad
        elif n < NE - 1:
            out_ref[...] += grad * grad
        else:
            out_ref[...] = (out_ref[...] + grad * grad) * (1.0 / NE)


def local(activations, out_grads, basis_in, basis_out, example_ids):
    feats, width = basis_in.shape
    outs = basis_out.shape[1]
    tokens = example_ids.shape[0]
    gk = out_grads.shape[1]
    gr = out_grads.shape[0] // 2
    vmem = pl.BlockSpec(memory_space=pltpu.VMEM)
    wide1 = (feats * 22 // 28) // 256 * 256
    correction = pl.pallas_call(
        functools.partial(exchange, wide1),
        out_shape=jax.ShapeDtypeStruct((width, outs), F32),
        in_specs=[vmem, vmem, pl.BlockSpec(memory_space=pl.ANY), vmem, vmem],
        out_specs=vmem,
        scratch_shapes=[
            pltpu.VMEM((tokens // ROWS, ROWS, width), BF),
            pltpu.VMEM((tokens // ROWS, ROWS, outs), BF),
            pltpu.VMEM((NY, 2, NZ, ROWS, feats), BF),
            pltpu.VMEM((width, feats), BF),
            pltpu.VMEM((NE * gr, 2 * gk), BF),
            pltpu.VMEM((2 * gk, outs), BF),
            pltpu.VMEM((NY, gr, outs), F32),
            pltpu.VMEM((2, NY // 2, gr, outs), F32),
            pltpu.VMEM((NZ, ROWS, outs), F32),
            pltpu.VMEM((NZ - 1, ROWS, outs), F32),
            pltpu.VMEM((2 * NZ * ROWS, width), F32),
            pltpu.VMEM((NY, ROWS, width), F32),
            pltpu.VMEM((NY, NE, ROWS, width), BF),
            pltpu.VMEM((NY, NE - 1, ROWS, width), BF),
            pltpu.SemaphoreType.DMA((320,)),
            pltpu.SemaphoreType.DMA((240,)),
            pltpu.SemaphoreType.DMA((1,)),
        ],
        compiler_params=pltpu.CompilerParams(
            collective_id=0, has_side_effects=True, vmem_limit_bytes=60 << 20
        ),
        name="exchange",
    )(activations, out_grads, basis_in.T, basis_out, example_ids.reshape(-1, 128))
    return correction.T


def solution(mesh):
    finer = Mesh(mesh.devices.reshape(2, NX, NZ, NY, 2), AXES)
    placed = (P(BLK, EX), P(EX, BLK), P(EX, BLK), P(BLK, EX), P())
    return jax.shard_map(local, mesh=finer, in_specs=placed, out_specs=P(EX, BLK), check_vma=False)
```
